32 devices in a mesh: section: 4 (over z), expert: 8 (over y, x, core).
Axes of the slice: x: 2, y: 2, z: 4, core: 2. Of those that a mesh axis runs over, the one named last changes fastest.
Arguments:
- activations: bfloat16 [4, 1024, 2048], P('section', 'expert'), may hold values from -6 to 6
- gradients: bfloat16 [4, 1024, 2048], P('section', 'expert'), may hold values from -6 to 6
- stashed: bfloat16 [4, 1024, 2048], P('section', 'expert'), may hold values from -6 to 6
- norm_gain: bfloat16 [4, 2048], P('section'), may hold values from 0.5 to 1.5
- router: bfloat16 [4, 2048, 8], P('section'), may hold values from -0.125 to 0.125
- gate_weight: bfloat16 [4, 8, 2048, 768], P('section', 'expert'), may hold values from -0.125 to 0.125
- up_weight: bfloat16 [4, 8, 2048, 768], P('section', 'expert'), may hold values from -0.125 to 0.125
- down_weight: bfloat16 [4, 8, 768, 2048], P('section', 'expert'), may hold values from -0.21875 to 0.21875
- routes_forward: int32 [4, 1024, 2], P('section', 'expert'), may hold values from 0 to 7, all different within a row; in each aligned block of 128 rows (0 to 127, 128 to 255, ..., all dimensions but the last counted through in order) at most 48 rows name the same one
- routes_backward: int32 [4, 1024, 2], P('section', 'expert'), may hold values from 0 to 7, all different within a row; in each aligned block of 128 rows (0 to 127, 128 to 255, ..., all dimensions but the last counted through in order) at most 48 rows name the same one
Outputs:
- layer_out: bfloat16 [4, 1024, 2048], P('section', 'expert')
- input_grad: bfloat16 [4, 1024, 2048], P('section', 'expert')
The draws below stay inside these ranges and needn't reach their ends.
Inputs may be any that keep to these rules, and one draw needn't show every extreme that they name: `routes_forward`: each token names 2 different experts. In each aligned block of 128 tokens (one index of expert's tokens of one section) no expert is named by more than 48 tokens, a bound that some block reaches. `routes_backward`: each token names 2 different experts. In each aligned block of 128 tokens (one index of expert's tokens of one section) no expert is named by more than 48 tokens, a bound that some block reaches.
All inputs are finite; a program needn't handle non-finite values.
Results may differ from the reference program's by a relative error of at most 0.0059.
Values may be sent and summed in bfloat16 or wider, within the bound.
A program may use at most 128 MiB of HBM per device.

```python
import math
from functools import partial
import jax
import jax.numpy as jnp
import numpy as np
from jax import lax

D = 2048
FF = 768
TOPK = 2
TOK_DEV = 128
SECTIONS = 4
EXPERTS = 8
TOKENS = 1024
CAP = 48
N_EXPERT = 8


def levels(key, shape, cuts, smallest, high):
    def one(axis_at, shards_of):
        draws = jax.random.uniform(jax.random.fold_in(jax.random.fold_in(key, 6), axis_at), (shards_of,), jnp.float32, smallest / len(cuts), high / len(cuts))
        return jnp.repeat(jnp.exp(draws), shape[axis_at] // shards_of).reshape((-1,) + (1,) * (len(shape) - axis_at - 1))

    gain = one(*cuts[0])
    for cut in cuts[1:]:
        gain = gain * one(*cut)
    return gain


def deal_out(stream_key, own, number, rows, count, top, limit, lean):
    ranking = jax.random.permutation(stream_key, count)
    crowded, common = shares(count, rows * top, limit, lean, True), shares(count, rows * top, limit, lean, False)
    places = jnp.arange(count)

    def named(tallies, offset_by):
        used = int((tallies > 0).sum())
        fixed = max(1, used // 4)
        passed = fixed + (places - fixed + offset_by * (used - fixed)) % max(1, count - fixed)
        return jnp.zeros((count,), jnp.int32).at[ranking[jnp.where(places < fixed, places, passed)]].set(jnp.asarray(tallies, jnp.int32))

    tallies = jnp.where(number % 4 == 0, named(crowded, number // 4), named(common, number - number // 4 - 1))
    mixed = jax.random.permutation(jax.random.fold_in(own, 3), count)
    source_of, sink = mixed[0:count // 2 * 2:2], mixed[1:count // 2 * 2:2]
    slack = jnp.minimum(tallies[source_of] - 1, limit - tallies[sink]) // 2
    slack = jnp.where((source_of == ranking[0]) | (sink == ranking[0]) | (tallies[sink] == 0), 0, jnp.maximum(slack, 0))
    passed = jax.random.randint(jax.random.fold_in(own, 4), (count // 2,), 0, 1 << 20) % (slack + 1)
    tallies = tallies.at[source_of].add(-passed).at[sink].add(passed)
    items = jnp.searchsorted(jnp.cumsum(tallies), jnp.arange(rows * top), side="right").astype(jnp.int32)
    grid = items.reshape(top, rows).T
    grid = grid[jax.random.permutation(jax.random.fold_in(own, 1), rows)]
    offset_by = jax.random.randint(jax.random.fold_in(own, 2), (rows, 1), 0, top)
    return jnp.take_along_axis(grid, (jnp.arange(top)[None, :] + offset_by) % top, axis=1)


def shares(count, total, most, skew, full):
    portions = [(1 << 20) // math.isqrt(rank ** skew) + 1 for rank in range(1, count + 1)]
    largest = most if full else min(most, max(-(-total // count), total * portions[0] // sum(portions)))
    least = 1 if total - largest >= count - 1 else 0
    holding, spare = [largest] + [least] * (count - 1), total - largest - least * (count - 1)
    while spare > 0:
        free = [i for i in range(1, count) if holding[i] < largest] or [i for i in range(1, count) if holding[i] < most]
        whole, left = sum([portions[i] for i in free]), spare
        for i in free:
            more = min(most - holding[i], max(1, left * portions[i] // whole), spare)
            holding[i] = holding[i] + more
            spare = spare - more
    return np.array(holding)


def centred(key, shape, scale, most, split=(), kind=jnp.bfloat16):
    values = jax.random.normal(key, shape, jnp.float32) * scale
    if len(split) > 0:
        values = levels(key, shape, split, -0.22, 0.18) * values
    return jnp.clip(values, min=-most, max=most).astype(kind)


def setup_inputs(seed: int = 0) -> dict:
    keys = jax.random.split(jax.random.key(seed), 11)
    activations = centred(keys[0], (SECTIONS, TOKENS, D), 1.0, 6.0, ((0, 4), (1, 8)))
    gradients = centred(keys[1], (SECTIONS, TOKENS, D), 1.0, 6.0, ((0, 4), (1, 8)))
    stashed = centred(keys[2], (SECTIONS, TOKENS, D), 1.0, 6.0, ((0, 4), (1, 8)))
    norm_gain = jnp.clip(1.0 + 0.1 * jax.random.normal(keys[3], (SECTIONS, D), jnp.float32), 0.5, 1.5).astype(jnp.bfloat16)
    router = centred(keys[4], (SECTIONS, D, EXPERTS), D ** -0.5, 0.125, ((0, 4),))
    gate_weight = centred(keys[5], (SECTIONS, EXPERTS, D, FF), D ** -0.5, 0.125, ((0, 4), (1, 8)))
    up_weight = centred(keys[6], (SECTIONS, EXPERTS, D, FF), D ** -0.5, 0.125, ((0, 4), (1, 8)))
    down_weight = centred(keys[7], (SECTIONS, EXPERTS, FF, D), FF ** -0.5, 0.21875, ((0, 4), (1, 8)))
    routes_forward_keys = jax.random.split(jax.random.fold_in(keys[8], 1), SECTIONS * TOKENS // TOK_DEV)
    routes_forward_turns = jax.random.permutation(jax.random.fold_in(keys[8], 3), SECTIONS * TOKENS // TOK_DEV)
    routes_forward = jax.vmap(lambda own, number: deal_out(jax.random.fold_in(keys[8], 2), own, number, TOK_DEV, EXPERTS, TOPK, CAP, 2))(routes_forward_keys, routes_forward_turns).reshape((SECTIONS, TOKENS, TOPK))
    routes_backward_keys = jax.random.split(jax.random.fold_in(keys[9], 1), SECTIONS * TOKENS // TOK_DEV)
    routes_backward_turns = jax.random.permutation(jax.random.fold_in(keys[9], 3), SECTIONS * TOKENS // TOK_DEV)
    routes_backward = jax.vmap(lambda own, number: deal_out(jax.random.fold_in(keys[9], 2), own, number, TOK_DEV, EXPERTS, TOPK, CAP, 2))(routes_backward_keys, routes_backward_turns).reshape((SECTIONS, TOKENS, TOPK))
    return {"activations": activations, "gradients": gradients, "stashed": stashed, "norm_gain": norm_gain, "router": router, "gate_weight": gate_weight, "up_weight": up_weight, "down_weight": down_weight, "routes_forward": routes_forward, "routes_backward": routes_backward}


NORM_EPS = 1e-06

def normalize(tokens, gain_row):
    values = tokens.astype(jnp.float32)
    inverse = lax.rsqrt(lax.optimization_barrier(jnp.mean(values * values, axis=-1, keepdims=True)) + NORM_EPS)
    normed = (values * inverse * gain_row.astype(jnp.float32)).astype(jnp.bfloat16)
    return (normed, inverse)

def route_weights(normed, router_mat, routes):
    logits = jnp.dot(normed, router_mat, preferred_element_type=jnp.float32)
    columns = jnp.arange(router_mat.shape[1], dtype=jnp.int32)
    matches = (routes[:, :, None] == columns[None, None, :]).astype(jnp.float32)
    picked = lax.optimization_barrier(jnp.sum(matches * logits[:, None, :], axis=2))
    sigmoids = jax.nn.sigmoid(picked)
    totals = lax.optimization_barrier(jnp.sum(sigmoids, axis=1, keepdims=True))
    return (sigmoids / totals, sigmoids, totals, matches)

def slot_positions(routes, expert_count, capacity):
    columns = jnp.arange(expert_count, dtype=jnp.int32)
    matches = (routes[:, :, None] == columns[None, None, :]).astype(jnp.int32)
    per_row = lax.optimization_barrier(jnp.sum(matches, axis=1))
    earlier = jnp.cumsum(per_row, axis=0) - per_row
    slots = lax.optimization_barrier(jnp.sum(matches * earlier[:, None, :], axis=2))
    return (routes * capacity + slots).astype(jnp.int32)

def dispatch_table(position, scales, slot_count):
    targets = jnp.arange(slot_count, dtype=jnp.int32)
    matches = position[None, :, :] == targets[:, None, None]
    return lax.optimization_barrier(jnp.sum(jnp.where(matches, scales[None, :, :], 0.0), axis=2)).astype(jnp.bfloat16)

def expert_forward(slot_rows, gate_mat, up_mat, down_mat):
    gate = jnp.dot(slot_rows, gate_mat, preferred_element_type=jnp.float32)
    upper = jnp.dot(slot_rows, up_mat, preferred_element_type=jnp.float32)
    hidden = (jax.nn.silu(gate) * upper).astype(jnp.bfloat16)
    result = jnp.dot(hidden, down_mat, preferred_element_type=jnp.float32).astype(jnp.bfloat16)
    return (result, gate, upper)

def expert_backward(slot_rows, slot_grad, gate_mat, up_mat, down_mat):
    result, gate, upper = expert_forward(slot_rows, gate_mat, up_mat, down_mat)
    dims = (((1,), (1,)), ((), ()))
    grad_hidden = lax.dot_general(slot_grad, down_mat, dims, preferred_element_type=jnp.float32)
    sigmoid_gate = jax.nn.sigmoid(gate)
    grad_up = (grad_hidden * gate * sigmoid_gate).astype(jnp.bfloat16)
    grad_gate = (grad_hidden * upper * sigmoid_gate * (1.0 + gate * (1.0 - sigmoid_gate))).astype(jnp.bfloat16)
    row_grad = lax.dot_general(grad_gate, gate_mat, dims, preferred_element_type=jnp.float32)
    row_grad = row_grad + lax.dot_general(grad_up, up_mat, dims, preferred_element_type=jnp.float32)
    return (result, row_grad.astype(jnp.bfloat16))

def router_backward(scores, weights, sigmoids, totals, matches, router_mat):
    mixed_score = lax.optimization_barrier(jnp.sum(weights * scores, axis=1, keepdims=True))
    grad_pick = (scores - mixed_score) / totals * sigmoids * (1.0 - sigmoids)
    grad_logits = lax.optimization_barrier(jnp.sum(grad_pick[:, :, None] * matches, axis=1))
    return jnp.dot(grad_logits, router_mat.astype(jnp.float32).T, precision=lax.Precision.HIGHEST)

def norm_backward(tokens, inverse, gain_row, grad_normed):
    values = tokens.astype(jnp.float32)
    grad_pre = grad_normed * gain_row.astype(jnp.float32)
    cubed = inverse * inverse * inverse
    return inverse * grad_pre - values * cubed * lax.optimization_barrier(jnp.mean(grad_pre * values, axis=-1, keepdims=True))

def forward_only(operands):
    slot_rows, gate_mat, up_mat, down_mat = operands
    return expert_forward(slot_rows, gate_mat, up_mat, down_mat)[0]

def backward_only(operands):
    slot_rows, slot_grad, gate_mat, up_mat, down_mat = operands
    return expert_backward(slot_rows, slot_grad, gate_mat, up_mat, down_mat)

def section_pass(operands):
    arrived, stored, cotangent, gain_row, router_mat, gate_all, up_all, down_all, route_front, route_back = operands
    sources = N_EXPERT
    experts = gate_all.shape[0]
    capacity = CAP
    slot_count = experts * capacity
    model_width = arrived.shape[1]
    per_source = arrived.shape[0] // sources

    def to_experts(buffers):
        shaped = buffers.reshape(sources, experts, capacity, model_width)
        return shaped.transpose(1, 0, 2, 3).reshape(experts, sources * capacity, model_width)

    def from_experts(outputs):
        shaped = outputs.reshape(experts, sources, capacity, model_width)
        return shaped.transpose(1, 0, 2, 3).reshape(sources, slot_count, model_width)

    def gather_slots(returned, position):
        picked = jax.vmap(partial(jnp.take, axis=0))(returned, position)
        return picked.reshape(sources * per_source, -1, model_width)

    def fill_slots(position, scales, tokens):
        tables = jax.vmap(partial(dispatch_table, slot_count=slot_count))(position, scales)
        grouped = tokens.reshape(sources, per_source, model_width)
        filled = jnp.einsum('njr,nrd->njd', tables.astype(jnp.float32), grouped.astype(jnp.float32))
        return filled.astype(jnp.bfloat16)
    locate = jax.vmap(partial(slot_positions, expert_count=experts, capacity=capacity))
    normed_f, inverse_f = normalize(arrived, gain_row)
    weights_f, sig_f, tot_f, match_f = route_weights(normed_f, router_mat, route_front)
    position_f = locate(route_front.reshape(sources, per_source, -1))
    unit_scales = jnp.ones(position_f.shape, jnp.float32)
    buffer_f = fill_slots(position_f, unit_scales, normed_f)
    outputs_f = lax.map(forward_only, (to_experts(buffer_f), gate_all, up_all, down_all))
    picked_f = gather_slots(from_experts(outputs_f), position_f)
    combined = lax.optimization_barrier(jnp.sum(weights_f[:, :, None] * picked_f.astype(jnp.float32), axis=1))
    layer_out = (arrived.astype(jnp.float32) + combined).astype(jnp.bfloat16)
    normed_b, inverse_b = normalize(stored, gain_row)
    weights_b, sig_b, tot_b, match_b = route_weights(normed_b, router_mat, route_back)
    position_b = locate(route_back.reshape(sources, per_source, -1))
    scale_round = lax.optimization_barrier(weights_b.astype(jnp.bfloat16)).astype(jnp.float32)
    buffer_b = fill_slots(position_b, unit_scales, normed_b)
    grad_buffer = fill_slots(position_b, scale_round.reshape(sources, per_source, -1), cotangent)
    outputs_b, grads_b = lax.map(backward_only, (to_experts(buffer_b), to_experts(grad_buffer), gate_all, up_all, down_all))
    picked_o = gather_slots(from_experts(outputs_b), position_b)
    picked_dn = gather_slots(from_experts(grads_b), position_b)
    scores = lax.optimization_barrier(jnp.sum(picked_o.astype(jnp.float32) * cotangent.astype(jnp.float32)[:, None, :], axis=2))
    scores = lax.optimization_barrier(scores.astype(jnp.bfloat16)).astype(jnp.float32)
    grad_normed = lax.optimization_barrier(jnp.sum(picked_dn.astype(jnp.float32), axis=1))
    grad_normed = grad_normed + router_backward(scores, weights_b, sig_b, tot_b, match_b, router_mat)
    input_grad = cotangent.astype(jnp.float32) + norm_backward(stored, inverse_b, gain_row, grad_normed)
    return (layer_out, input_grad.astype(jnp.bfloat16))

def reference(activations, gradients, stashed, norm_gain, router, gate_weight, up_weight, down_weight, routes_forward, routes_backward):
    arrived = jnp.roll(activations, 1, axis=0)
    cotangents = jnp.roll(gradients, -1, axis=0)
    layer_out, input_grad = lax.map(section_pass, (arrived, stashed, cotangents, norm_gain, router, gate_weight, up_weight, down_weight, routes_forward, routes_backward))
    return (layer_out, input_grad)
```

```python
import functools

import jax
import jax.numpy as jnp
from jax import lax
from jax.experimental import pallas as pl
from jax.experimental.pallas import tpu as pltpu
from jax.sharding import PartitionSpec as P

NORM_EPS = 1e-06
LANES = 128
CHUNK = 256
F32, BF16 = jnp.float32, jnp.bfloat16
MESH = pl.DeviceIdType.MESH
NN = (((1,), (0,)), ((), ()))
NT = (((1,), (1,)), ((), ()))
ROW_B, ROW_C, ROW_F, OUT_G, OUT_F = range(5)


def mm(left, right, dims=NN):
    return lax.dot_general(left, right, dims, preferred_element_type=F32)


def halves(value):
    high = value.astype(BF16)
    return high, (value - high.astype(F32)).astype(BF16)


def chunks(width, step, work):
    @pl.loop(0, width // step)
    def _(index):
        work(pl.ds(pl.multiple_of(index * step, step), step))


def inverse_rms(values):
    return lax.rsqrt(jnp.mean(values * values, axis=1, keepdims=True) + NORM_EPS)


def places(routes, top, capacity):
    rows = routes.shape[0]
    columns = lax.broadcasted_iota(jnp.int32, (rows, LANES), 1)
    matches = [(routes[:, k : k + 1] == columns).astype(F32) for k in range(top)]
    per_row = sum(matches)
    before = lax.broadcasted_iota(jnp.int32, (rows, rows), 1) < lax.broadcasted_iota(
        jnp.int32, (rows, rows), 0
    )
    earlier = mm(before.astype(F32).astype(BF16), per_row.astype(BF16))
    offsets = earlier + columns.astype(F32) * capacity
    return matches, [jnp.sum(m * offsets, axis=1, keepdims=True) for m in matches]


def route_weights(normed, router, matches):
    logits = mm(normed, router)
    sig = [jax.nn.sigmoid(jnp.sum(m * logits, axis=1, keepdims=True)) for m in matches]
    total = sum(sig)
    return [s / total for s in sig], sig, total


def table(positions, scales, slots):
    rows = positions[0].shape[0]
    columns = lax.broadcasted_iota(jnp.int32, (rows, slots), 1).astype(F32)
    return sum(jnp.where(columns == p, s, 0.0) for p, s in zip(positions, scales))


def kernel(
    owners, sections, capacity, top,
    act_ref, grad_ref, stored_ref, gain_ref, router_ref, routes_f_ref, routes_b_ref,
    gate_hbm, up_hbm, down_hbm,
    layer_ref, input_ref,
    gate_w, up_w, down_w, arrived, cot,
    send_b, send_c, send_f, send_g, send_o,
    recv_b, recv_c, recv_f, recv_g, recv_o,
    normed, gate, upper, hidden, slot_grad, out_b, grad_gate, grad_up, acc,
    weight_sem, hop_send, hop_recv, send_sem, recv_sem,
):
    slots = owners * capacity
    width = act_ref.shape[1]
    hidden_width = gate_w.shape[1]
    me = lax.axis_index("expert")
    section = lax.axis_index("section")
    after = lax.rem(section + 1, sections)
    before = lax.rem(section + sections - 1, sections)
    sends = (send_b, send_c, send_f, send_g, send_o)
    recvs = (recv_b, recv_c, recv_f, recv_g, recv_o)

    loads = [
        pltpu.make_async_copy(source, target, weight_sem.at[i])
        for i, (source, target) in enumerate(
            ((gate_hbm, gate_w), (up_hbm, up_w), (down_hbm, down_w))
        )
    ]
    for load in loads:
        load.start()

    barrier = pltpu.get_barrier_semaphore()

    @pl.loop(1, owners)
    def _(step):
        pl.semaphore_signal(
            barrier, inc=1, device_id={"expert": lax.rem(me + step, owners)}, device_id_type=MESH
        )

    for neighbour in (after, before):
        pl.semaphore_signal(barrier, inc=1, device_id={"section": neighbour}, device_id_type=MESH)
    pl.semaphore_wait(barrier, owners + 1)

    def rows_of(index):
        return pl.ds(pl.multiple_of(index * capacity, 16), capacity)

    def block_copy(kind, step):
        peer = lax.rem(me + step, owners)
        return pltpu.make_async_remote_copy(
            src_ref=sends[kind].at[rows_of(peer)],
            dst_ref=recvs[kind].at[rows_of(me)],
            send_sem=send_sem.at[kind, step],
            recv_sem=recv_sem.at[kind, step],
            device_id={"expert": peer},
            device_id_type=MESH,
        )

    def send(kind):
        @pl.loop(1, owners)
        def _(step):
            block_copy(kind, step).start()

        recvs[kind][rows_of(me)] = sends[kind][rows_of(me)]

    def receive(kind):
        @pl.loop(1, owners)
        def _(step):
            source = lax.rem(me + owners - step, owners)
            pltpu.make_async_remote_copy(
                src_ref=sends[kind].at[rows_of(source)],
                dst_ref=recvs[kind].at[rows_of(source)],
                send_sem=send_sem.at[kind, step],
                recv_sem=recv_sem.at[kind, step],
                device_id={"expert": source},
                device_id_type=MESH,
            ).wait_recv()

    def hop(index, source, target, neighbour):
        return pltpu.make_async_remote_copy(
            src_ref=source, dst_ref=target,
            send_sem=hop_send.at[index], recv_sem=hop_recv.at[index],
            device_id={"section": neighbour}, device_id_type=MESH,
        )

    grad_hop = hop(0, grad_ref, cot, before)
    act_hop = hop(1, act_ref, arrived, after)
    grad_hop.start()

    gain = gain_ref[...].astype(F32)
    router = router_ref[...]
    ones = [1.0] * top

    match_b, pos_b = places(routes_b_ref[...], top, capacity)
    values = stored_ref[...].astype(F32)
    inverse_b = inverse_rms(values)
    normed[...] = (values * inverse_b * gain).astype(BF16)
    spread_b = table(pos_b, ones, slots).T.astype(BF16)

    def fill_b(cols):
        send_b[:, cols] = mm(spread_b, normed[:, cols]).astype(BF16)

    chunks(width, CHUNK, fill_b)
    send(ROW_B)
    weights_b, sig_b, total_b = route_weights(normed[...], router, match_b)
    scales = [w.astype(BF16).astype(F32) for w in weights_b]
    scale_table = table(pos_b, scales, slots).T.astype(BF16)
    send_c[:, width:] = mm(scale_table, jnp.ones((scale_table.shape[1], LANES), BF16)).astype(BF16)

    grad_hop.wait()
    act_hop.start()

    def fill_c(cols):
        send_c[:, cols] = mm(spread_b, cot[:, cols]).astype(BF16)

    chunks(width, CHUNK, fill_c)
    send(ROW_C)

    def expert_hidden(rows_ref, keep):
        def work(cols):
            g = mm(rows_ref[...], gate_w[:, cols])
            u = mm(rows_ref[...], up_w[:, cols])
            if keep:
                gate[:, cols] = g
                upper[:, cols] = u
            hidden[:, cols] = (g * jax.nn.sigmoid(g) * u).astype(BF16)

        chunks(hidden_width, CHUNK, work)

    def expert_down(target):
        def work(cols):
            target[:, cols] = mm(hidden[...], down_w[:, cols]).astype(BF16)

        chunks(width, CHUNK, work)

    for load in loads:
        load.wait()
    receive(ROW_B)
    expert_hidden(recv_b, True)

    match_f, pos_f = places(routes_f_ref[...], top, capacity)
    spread_f = table(pos_f, ones, slots).T.astype(BF16)
    act_hop.wait()
    values = arrived[...].astype(F32)
    normed[...] = (values * inverse_rms(values) * gain).astype(BF16)

    def fill_f(cols):
        send_f[:, cols] = mm(spread_f, normed[:, cols]).astype(BF16)

    chunks(width, CHUNK, fill_f)
    send(ROW_F)
    weights_f = route_weights(normed[...], router, match_f)[0]
    expert_down(out_b)

    receive(ROW_C)
    acc[...] = jnp.zeros_like(acc)
    scale = recv_c[:, width:].astype(F32)[:, :1]

    def scale_rows(cols):
        rows = recv_c[:, cols].astype(F32)
        slot_grad[:, cols] = (scale * rows).astype(BF16)
        product = rows * out_b[:, cols].astype(F32)
        acc[...] += product[:, :LANES] + product[:, LANES:]

    chunks(width, CHUNK, scale_rows)

    def hidden_grads(cols):
        grad_hidden = mm(slot_grad[...], down_w[cols, :], NT)
        g = gate[:, cols]
        s = jax.nn.sigmoid(g)
        grad_up[:, cols] = (grad_hidden * g * s).astype(BF16)
        grad_gate[:, cols] = (
            grad_hidden * upper[:, cols] * s * (1.0 + g * (1.0 - s))
        ).astype(BF16)

    chunks(hidden_width, CHUNK, hidden_grads)

    def row_grads(cols):
        total = mm(grad_gate[...], gate_w[cols, :], NT) + mm(grad_up[...], up_w[cols, :], NT)
        send_g[:, cols] = total.astype(BF16)

    chunks(width, CHUNK, row_grads)
    scores = jnp.sum(acc[...], axis=1, keepdims=True)
    send_g[:, width:] = jnp.broadcast_to(scores, (slots, LANES)).astype(BF16)
    send(OUT_G)

    receive(ROW_F)
    expert_hidden(recv_f, False)
    expert_down(send_o)
    send(OUT_F)

    receive(OUT_G)
    score = [
        mm(table([p], [1.0], slots).astype(BF16), recv_g[:, width:])[:, :1] for p in pos_b
    ]
    mixed = sum(w * s for w, s in zip(weights_b, score))
    grad_logits = sum(
        (s - mixed) / total_b * g * (1.0 - g) * m for s, g, m in zip(score, sig_b, match_b)
    )
    logits_high, logits_low = halves(grad_logits)
    gather_b = table(pos_b, ones, slots).astype(BF16)
    grad_normed = (
        mm(gather_b, recv_g[:, :width])
        + mm(logits_high, router, NT)
        + mm(logits_low, router, NT)
    )
    grad_pre = grad_normed * gain
    values = stored_ref[...].astype(F32)
    mean = jnp.mean(grad_pre * values, axis=1, keepdims=True)
    input_ref[...] = (
        cot[...].astype(F32)
        + inverse_b * grad_pre
        - values * (inverse_b * inverse_b * inverse_b) * mean
    ).astype(BF16)

    weight_high, weight_low = halves(table(pos_f, weights_f, slots))
    receive(OUT_F)

    def combine(cols):
        rows = recv_o[:, cols]
        mixed_rows = mm(weight_high, rows) + mm(weight_low, rows)
        layer_ref[:, cols] = (arrived[:, cols].astype(F32) + mixed_rows).astype(BF16)

    chunks(width, CHUNK, combine)

    for kind in range(5):

        @pl.loop(1, owners)
        def _(step, kind=kind):
            block_copy(kind, step).wait_send()


def body(
    activations, gradients, stashed, norm_gain, router,
    gate_weight, up_weight, down_weight, routes_forward, routes_backward,
):
    owners, sections = lax.axis_size("expert"), lax.axis_size("section")
    rows, width = activations.shape[1:]
    top = routes_forward.shape[2]
    hidden_width = gate_weight.shape[3]
    capacity = 3 * rows * top // (2 * owners)
    capacity = -(-capacity // 16) * 16
    slots = owners * capacity
    router_mat = jnp.pad(router[0], ((0, 0), (0, LANES - router.shape[2])))
    vmem, hbm = pl.BlockSpec(memory_space=pltpu.VMEM), pl.BlockSpec(memory_space=pl.ANY)
    plain, wide = pltpu.VMEM((slots, width), BF16), pltpu.VMEM((slots, width + LANES), BF16)
    inner = pltpu.VMEM((slots, hidden_width), BF16)
    inner_f32 = pltpu.VMEM((slots, hidden_width), F32)
    tokens = pltpu.VMEM((rows, width), BF16)
    layer_out, input_grad = pl.pallas_call(
        functools.partial(kernel, owners, sections, capacity, top),
        out_shape=[jax.ShapeDtypeStruct((rows, width), BF16)] * 2,
        in_specs=[vmem] * 7 + [hbm] * 3,
        out_specs=[vmem] * 2,
        scratch_shapes=[
            pltpu.VMEM((width, hidden_width), BF16),
            pltpu.VMEM((width, hidden_width), BF16),
            pltpu.VMEM((hidden_width, width), BF16),
            tokens, tokens,
            plain, wide, plain, wide, plain,
            plain, wide, plain, wide, plain,
            tokens, inner_f32, inner_f32, inner, plain, plain, inner, inner,
            pltpu.VMEM((slots, LANES), F32),
            pltpu.SemaphoreType.DMA((3,)),
            pltpu.SemaphoreType.DMA((2,)),
            pltpu.SemaphoreType.DMA((2,)),
            pltpu.SemaphoreType.DMA((5, owners)),
            pltpu.SemaphoreType.DMA((5, owners)),
        ],
        compiler_params=pltpu.CompilerParams(
            collective_id=0, has_side_effects=True, vmem_limit_bytes=58 << 20
        ),
        cost_estimate=pl.CostEstimate(
            flops=18 * slots * width * hidden_width,
            bytes_accessed=6 * width * hidden_width + 10 * rows * width,
            transcendentals=3 * slots * hidden_width,
        ),
    )(
        activations[0], gradients[0], stashed[0], norm_gain, router_mat,
        routes_forward[0], routes_backward[0],
        gate_weight[0, 0], up_weight[0, 0], down_weight[0, 0],
    )
    return layer_out[None], input_grad[None]


def solution(mesh):
    rows = P("section", "expert", None)
    experts = P("section", "expert", None, None)
    placed = (
        rows, rows, rows, P("section", None), P("section", None, None),
        experts, experts, experts, rows, rows,
    )
    return jax.shard_map(
        body, mesh=mesh, in_specs=placed, out_specs=(rows, rows), check_vma=False
    )
```

```python
import functools

import jax
import jax.numpy as jnp
from jax import lax
from jax.experimental import pallas as pl
from jax.experimental.pallas import tpu as pltpu
from jax.sharding import PartitionSpec as P

NORM_EPS = 1e-06
LANES = 128
CHUNK = 256
F32, BF16 = jnp.float32, jnp.bfloat16
MESH = pl.DeviceIdType.MESH
NN = (((1,), (0,)), ((), ()))
NT = (((1,), (1,)), ((), ()))
ROW_B, ROW_C, ROW_F, OUT_G, OUT_F = range(5)


def mm(left, right, dims=NN):
    return lax.dot_general(left, right, dims, preferred_element_type=F32)


def halves(value):
    high = value.astype(BF16)
    return high, (value - high.astype(F32)).astype(BF16)


def chunks(width, step, work):
    @pl.loop(0, width // step)
    def _(index):
        work(pl.ds(pl.multiple_of(index * step, step), step))


def inverse_rms(values):
    return lax.rsqrt(jnp.mean(values * values, axis=1, keepdims=True) + NORM_EPS)


def places(routes, top, capacity):
    rows = routes.shape[1]
    columns = lax.broadcasted_iota(jnp.int32, (rows, LANES), 1).astype(F32)
    across = lax.broadcasted_iota(jnp.int32, (rows, rows), 1)
    down = lax.broadcasted_iota(jnp.int32, (rows, rows), 0)
    named = [
        jnp.sum(
            jnp.where(across == down, routes[k : k + 1, :].astype(F32), 0.0),
            axis=1, keepdims=True,
        )
        for k in range(top)
    ]
    matches = [(n == columns).astype(F32) for n in named]
    per_row = sum(matches)
    before = across < down
    earlier = mm(before.astype(F32).astype(BF16), per_row.astype(BF16))
    offsets = earlier + columns * capacity
    return matches, [jnp.sum(m * offsets, axis=1, keepdims=True) for m in matches]


def route_weights(normed, router, matches):
    logits = mm(normed, router, NT)
    sig = [jax.nn.sigmoid(jnp.sum(m * logits, axis=1, keepdims=True)) for m in matches]
    total = sum(sig)
    return [s / total for s in sig], sig, total


def table(positions, scales, slots):
    rows = positions[0].shape[0]
    columns = lax.broadcasted_iota(jnp.int32, (rows, slots), 1).astype(F32)
    return sum(jnp.where(columns == p, s, 0.0) for p, s in zip(positions, scales))


def kernel(
    owners, sections, capacity, top,
    act_ref, grad_ref, stored_ref, gain_ref, router_ref, routes_f_ref, routes_b_ref,
    gate_hbm, up_hbm, down_hbm,
    layer_ref, input_ref,
    gate_w, up_w, down_w, arrived, cot,
    send_b, send_c, send_f, send_g, send_o,
    recv_b, recv_c, recv_f, recv_g, recv_o,
    normed, gate, upper, hidden, slot_grad, out_b, grad_gate, grad_up, acc,
    weight_sem, hop_send, hop_recv, send_sem, recv_sem,
):
    slots = owners * capacity
    width = act_ref.shape[1]
    hidden_width = gate_w.shape[1]
    me = lax.axis_index("expert")
    section = lax.axis_index("section")
    after = lax.rem(section + 1, sections)
    before = lax.rem(section + sections - 1, sections)
    sends = (send_b, send_c, send_f, send_g, send_o)
    recvs = (recv_b, recv_c, recv_f, recv_g, recv_o)

    loads = [
        pltpu.make_async_copy(source, target, weight_sem.at[i])
        for i, (source, target) in enumerate(
            ((gate_hbm, gate_w), (up_hbm, up_w), (down_hbm, down_w))
        )
    ]
    for load in loads:
        load.start()

    barrier = pltpu.get_barrier_semaphore()

    @pl.loop(1, owners)
    def _(step):
        pl.semaphore_signal(
            barrier, inc=1, device_id={"expert": lax.rem(me + step, owners)}, device_id_type=MESH
        )

    for neighbour in (after, before):
        pl.semaphore_signal(barrier, inc=1, device_id={"section": neighbour}, device_id_type=MESH)
    def rows_of(index):
        return pl.ds(pl.multiple_of(index * capacity, 16), capacity)

    def block_copy(kind, step):
        peer = lax.rem(me + step, owners)
        return pltpu.make_async_remote_copy(
            src_ref=sends[kind].at[rows_of(peer)],
            dst_ref=recvs[kind].at[rows_of(me)],
            send_sem=send_sem.at[kind, step],
            recv_sem=recv_sem.at[kind, step],
            device_id={"expert": peer},
            device_id_type=MESH,
        )

    def send(kind):
        @pl.loop(1, owners)
        def _(step):
            block_copy(kind, step).start()

        recvs[kind][rows_of(me)] = sends[kind][rows_of(me)]

    def receive(kind):
        @pl.loop(1, owners)
        def _(step):
            source = lax.rem(me + owners - step, owners)
            pltpu.make_async_remote_copy(
                src_ref=sends[kind].at[rows_of(source)],
                dst_ref=recvs[kind].at[rows_of(source)],
                send_sem=send_sem.at[kind, step],
                recv_sem=recv_sem.at[kind, step],
                device_id={"expert": source},
                device_id_type=MESH,
            ).wait_recv()

    def hop(index, source, target, neighbour):
        return pltpu.make_async_remote_copy(
            src_ref=source, dst_ref=target,
            send_sem=hop_send.at[index], recv_sem=hop_recv.at[index],
            device_id={"section": neighbour}, device_id_type=MESH,
        )

    grad_hop = hop(0, grad_ref, cot, before)
    act_hop = hop(1, act_ref, arrived, after)
    gain = gain_ref[...].astype(F32)
    experts = router_ref.shape[0]
    router = jnp.concatenate(
        [router_ref[...].astype(F32), jnp.zeros((LANES - experts, width), F32)], axis=0
    ).astype(BF16)
    ones = [1.0] * top

    match_b, pos_b = places(routes_b_ref[...], top, capacity)
    values = stored_ref[...].astype(F32)
    inverse_b = inverse_rms(values)
    normed[...] = (values * inverse_b * gain).astype(BF16)
    spread_b = table(pos_b, ones, slots).T.astype(BF16)

    def fill_b(cols):
        send_b[:, cols] = mm(spread_b, normed[:, cols]).astype(BF16)

    chunks(width, CHUNK, fill_b)
    pl.semaphore_wait(barrier, owners + 1)
    grad_hop.start()
    send(ROW_B)
    weights_b, sig_b, total_b = route_weights(normed[...], router, match_b)
    scales = [w.astype(BF16).astype(F32) for w in weights_b]
    scale_table = table(pos_b, scales, slots).T.astype(BF16)
    send_c[:, width:] = mm(scale_table, jnp.ones((scale_table.shape[1], LANES), BF16)).astype(BF16)

    grad_hop.wait()
    act_hop.start()

    def fill_c(cols):
        send_c[:, cols] = mm(spread_b, cot[:, cols]).astype(BF16)

    chunks(width, CHUNK, fill_c)
    send(ROW_C)

    def expert_hidden(rows_ref, keep):
        def work(cols):
            g = mm(rows_ref[...], gate_w[:, cols])
            u = mm(rows_ref[...], up_w[:, cols])
            if keep:
                gate[:, cols] = g
                upper[:, cols] = u
            hidden[:, cols] = (g * jax.nn.sigmoid(g) * u).astype(BF16)

        chunks(hidden_width, CHUNK, work)

    def expert_down(target):
        def work(cols):
            target[:, cols] = mm(hidden[...], down_w[:, cols]).astype(BF16)

        chunks(width, CHUNK, work)

    match_f, pos_f = places(routes_f_ref[...], top, capacity)
    spread_f = table(pos_f, ones, slots).T.astype(BF16)
    act_hop.wait()
    values = arrived[...].astype(F32)
    normed[...] = (values * inverse_rms(values) * gain).astype(BF16)

    def fill_f(cols):
        send_f[:, cols] = mm(spread_f, normed[:, cols]).astype(BF16)

    chunks(width, CHUNK, fill_f)
    weights_f = route_weights(normed[...], router, match_f)[0]
    for load in loads:
        load.wait()
    receive(ROW_B)
    send(ROW_F)
    expert_hidden(recv_b, True)
    expert_down(out_b)

    receive(ROW_C)
    acc[...] = jnp.zeros_like(acc)
    scale = recv_c[:, width:].astype(F32)[:, :1]

    def scale_rows(cols):
        rows = recv_c[:, cols].astype(F32)
        slot_grad[:, cols] = (scale * rows).astype(BF16)
        product = rows * out_b[:, cols].astype(F32)
        acc[...] += product[:, :LANES] + product[:, LANES:]

    chunks(width, CHUNK, scale_rows)

    def hidden_grads(cols):
        grad_hidden = mm(slot_grad[...], down_w[cols, :], NT)
        g = gate[:, cols]
        s = jax.nn.sigmoid(g)
        grad_up[:, cols] = (grad_hidden * g * s).astype(BF16)
        grad_gate[:, cols] = (
            grad_hidden * upper[:, cols] * s * (1.0 + g * (1.0 - s))
        ).astype(BF16)

    chunks(hidden_width, CHUNK, hidden_grads)

    def row_grads(cols):
        total = mm(grad_gate[...], gate_w[cols, :], NT) + mm(grad_up[...], up_w[cols, :], NT)
        send_g[:, cols] = total.astype(BF16)

    chunks(width, CHUNK, row_grads)
    scores = jnp.sum(acc[...], axis=1, keepdims=True)
    send_g[:, width:] = jnp.broadcast_to(scores, (slots, LANES)).astype(BF16)
    send(OUT_G)

    receive(ROW_F)
    expert_hidden(recv_f, False)
    expert_down(send_o)
    send(OUT_F)

    receive(OUT_G)
    score = [
        mm(table([p], [1.0], slots).astype(BF16), recv_g[:, width:])[:, :1] for p in pos_b
    ]
    mixed = sum(w * s for w, s in zip(weights_b, score))
    grad_logits = sum(
        (s - mixed) / total_b * g * (1.0 - g) * m for s, g, m in zip(score, sig_b, match_b)
    )
    logits_high, logits_low = halves(grad_logits)
    gather_b = table(pos_b, ones, slots).astype(BF16)
    grad_normed = (
        mm(gather_b, recv_g[:, :width])
        + mm(logits_high, router)
        + mm(logits_low, router)
    )
    grad_pre = grad_normed * gain
    values = stored_ref[...].astype(F32)
    mean = jnp.mean(grad_pre * values, axis=1, keepdims=True)
    input_ref[...] = (
        cot[...].astype(F32)
        + inverse_b * grad_pre
        - values * (inverse_b * inverse_b * inverse_b) * mean
    ).astype(BF16)

    weight_high, weight_low = halves(table(pos_f, weights_f, slots))
    receive(OUT_F)

    def combine(cols):
        rows = recv_o[:, cols]
        mixed_rows = mm(weight_high, rows) + mm(weight_low, rows)
        layer_ref[:, cols] = (arrived[:, cols].astype(F32) + mixed_rows).astype(BF16)

    chunks(width, CHUNK, combine)

    for kind in range(5):

        @pl.loop(1, owners)
        def _(step, kind=kind):
            block_copy(kind, step).wait_send()


def hand_over(layer_in, grad_in, layer_ref, input_ref):
    layer_ref[...] = layer_in[...]
    input_ref[...] = grad_in[...]


def body(
    activations, gradients, stashed, norm_gain, router,
    gate_weight, up_weight, down_weight, routes_forward, routes_backward,
):
    owners, sections = lax.axis_size("expert"), lax.axis_size("section")
    rows, width = activations.shape[1:]
    top = routes_forward.shape[2]
    hidden_width = gate_weight.shape[3]
    capacity = 3 * rows * top // (2 * owners)
    capacity = -(-capacity // 16) * 16
    slots = owners * capacity
    vmem, hbm = pl.BlockSpec(memory_space=pltpu.VMEM), pl.BlockSpec(memory_space=pl.ANY)
    plain, wide = pltpu.VMEM((slots, width), BF16), pltpu.VMEM((slots, width + LANES), BF16)
    inner = pltpu.VMEM((slots, hidden_width), BF16)
    inner_f32 = pltpu.VMEM((slots, hidden_width), F32)
    tokens = pltpu.VMEM((rows, width), BF16)
    layer_out, input_grad = pl.pallas_call(
        functools.partial(kernel, owners, sections, capacity, top),
        out_shape=[jax.ShapeDtypeStruct((rows, width), BF16)] * 2,
        in_specs=[vmem] * 7 + [hbm] * 3,
        out_specs=[vmem] * 2,
        scratch_shapes=[
            pltpu.VMEM((width, hidden_width), BF16),
            pltpu.VMEM((width, hidden_width), BF16),
            pltpu.VMEM((hidden_width, width), BF16),
            tokens, tokens,
            plain, wide, plain, wide, plain,
            plain, wide, plain, wide, plain,
            tokens, inner_f32, inner_f32, inner, plain, plain, inner, inner,
            pltpu.VMEM((slots, LANES), F32),
            pltpu.SemaphoreType.DMA((3,)),
            pltpu.SemaphoreType.DMA((2,)),
            pltpu.SemaphoreType.DMA((2,)),
            pltpu.SemaphoreType.DMA((5, owners)),
            pltpu.SemaphoreType.DMA((5, owners)),
        ],
        compiler_params=pltpu.CompilerParams(
            collective_id=0, has_side_effects=True, vmem_limit_bytes=58 << 20
        ),
        cost_estimate=pl.CostEstimate(
            flops=18 * slots * width * hidden_width,
            bytes_accessed=6 * width * hidden_width + 10 * rows * width,
            transcendentals=3 * slots * hidden_width,
        ),
    )(
        activations[0], gradients[0], stashed[0], norm_gain, router[0].T,
        routes_forward[0].T, routes_backward[0].T,
        gate_weight[0, 0], up_weight[0, 0], down_weight[0, 0],
    )
    layer_out, input_grad = pl.pallas_call(
        hand_over,
        grid=(rows // 32,),
        out_shape=[jax.ShapeDtypeStruct((rows, width), BF16)] * 2,
        in_specs=[pl.BlockSpec((32, width), lambda i: (i, 0))] * 2,
        out_specs=[pl.BlockSpec((32, width), lambda i: (i, 0))] * 2,
    )(layer_out, input_grad)
    return layer_out[None], input_grad[None]


def solution(mesh):
    rows = P("section", "expert", None)
    experts = P("section", "expert", None, None)
    placed = (
        rows, rows, rows, P("section", None), P("section", None, None),
        experts, experts, experts, rows, rows,
    )
    return jax.shard_map(
        body, mesh=mesh, in_specs=placed, out_specs=(rows, rows), check_vma=False
    )
```

```python
import functools

import jax
import jax.numpy as jnp
from jax import lax
from jax.experimental import pallas as pl
from jax.experimental.pallas import tpu as pltpu
from jax.sharding import PartitionSpec as P

NORM_EPS = 1e-06
LANES = 128
CHUNK = 256
F32, BF16 = jnp.float32, jnp.bfloat16
MESH = pl.DeviceIdType.MESH
NN = (((1,), (0,)), ((), ()))
NT = (((1,), (1,)), ((), ()))
ROW_B, ROW_C, ROW_F, OUT_G, OUT_F = range(5)


def mm(left, right, dims=NN):
    return lax.dot_general(left, right, dims, preferred_element_type=F32)


def halves(value):
    high = value.astype(BF16)
    return high, (value - high.astype(F32)).astype(BF16)


def chunks(start, stop, step, work):
    @pl.loop(start // step, stop // step)
    def _(index):
        work(pl.ds(pl.multiple_of(index * step, step), step))


def inverse_rms(values):
    return lax.rsqrt(jnp.mean(values * values, axis=1, keepdims=True) + NORM_EPS)


def places(routes, top, capacity):
    rows = routes.shape[1]
    columns = lax.broadcasted_iota(jnp.int32, (rows, LANES), 1).astype(F32)
    across = lax.broadcasted_iota(jnp.int32, (rows, rows), 1)
    down = lax.broadcasted_iota(jnp.int32, (rows, rows), 0)
    named = [
        jnp.sum(
            jnp.where(across == down, routes[k : k + 1, :].astype(F32), 0.0),
            axis=1, keepdims=True,
        )
        for k in range(top)
    ]
    matches = [(n == columns).astype(F32) for n in named]
    per_row = sum(matches)
    before = across < down
    earlier = mm(before.astype(F32).astype(BF16), per_row.astype(BF16))
    offsets = earlier + columns * capacity
    return matches, [jnp.sum(m * offsets, axis=1, keepdims=True) for m in matches]


def route_weights(normed, router, matches):
    logits = mm(normed, router, NT)
    sig = [jax.nn.sigmoid(jnp.sum(m * logits, axis=1, keepdims=True)) for m in matches]
    total = sum(sig)
    return [s / total for s in sig], sig, total


def table(positions, scales, slots):
    rows = positions[0].shape[0]
    columns = lax.broadcasted_iota(jnp.int32, (rows, slots), 1).astype(F32)
    return sum(jnp.where(columns == p, s, 0.0) for p, s in zip(positions, scales))


def kernel(
    owners, sections, capacity, top,
    act_ref, grad_ref, stored_ref, gain_ref, router_ref, routes_f_ref, routes_b_ref,
    gate_hbm, up_hbm, down_hbm,
    layer_ref, input_ref,
    gate_w, up_w, down_w, arrived, cot,
    send_b, send_c, send_f, send_g, send_o,
    recv_b, recv_c, recv_f, recv_g, recv_o,
    normed, gate, upper, hidden, slot_grad, out_b, grad_gate, grad_up, acc,
    weight_sem, hop_send, hop_recv, send_sem, recv_sem,
):
    slots = owners * capacity
    width = act_ref.shape[1]
    hidden_width = gate_w.shape[1]
    me = lax.axis_index("expert")
    section = lax.axis_index("section")
    after = lax.rem(section + 1, sections)
    before = lax.rem(section + sections - 1, sections)
    sends = (send_b, send_c, send_f, send_g, send_o)
    recvs = (recv_b, recv_c, recv_f, recv_g, recv_o)

    loads = [
        pltpu.make_async_copy(source, target, weight_sem.at[i])
        for i, (source, target) in enumerate(
            ((gate_hbm, gate_w), (up_hbm, up_w), (down_hbm, down_w))
        )
    ]
    for load in loads:
        load.start()

    barrier = pltpu.get_barrier_semaphore()

    @pl.loop(1, owners)
    def _(step):
        pl.semaphore_signal(
            barrier, inc=1, device_id={"expert": lax.rem(me + step, owners)}, device_id_type=MESH
        )

    for neighbour in (after, before):
        pl.semaphore_signal(barrier, inc=1, device_id={"section": neighbour}, device_id_type=MESH)
    def rows_of(index):
        return pl.ds(pl.multiple_of(index * capacity, 16), capacity)

    half = width // 2

    def columns_of(kind, part):
        stop = sends[kind].shape[1] if part else half
        return pl.ds(part * half, stop - part * half)

    def block_copy(kind, part, step):
        peer = lax.rem(me + step, owners)
        cols = columns_of(kind, part)
        return pltpu.make_async_remote_copy(
            src_ref=sends[kind].at[rows_of(peer), cols],
            dst_ref=recvs[kind].at[rows_of(me), cols],
            send_sem=send_sem.at[2 * kind + part, step],
            recv_sem=recv_sem.at[2 * kind + part, step],
            device_id={"expert": peer},
            device_id_type=MESH,
        )

    def send(kind, part):
        @pl.loop(1, owners)
        def _(step):
            block_copy(kind, part, step).start()

        cols = columns_of(kind, part)
        recvs[kind][rows_of(me), cols] = sends[kind][rows_of(me), cols]

    def fill_and_send(kind, work):
        for part in range(2):
            chunks(part * half, (part + 1) * half, CHUNK, work)
            send(kind, part)

    def receive(kind, part):
        cols = columns_of(kind, part)

        @pl.loop(1, owners)
        def _(step):
            source = lax.rem(me + owners - step, owners)
            pltpu.make_async_remote_copy(
                src_ref=sends[kind].at[rows_of(source), cols],
                dst_ref=recvs[kind].at[rows_of(source), cols],
                send_sem=send_sem.at[2 * kind + part, step],
                recv_sem=recv_sem.at[2 * kind + part, step],
                device_id={"expert": source},
                device_id_type=MESH,
            ).wait_recv()

    def hop(index, source, target, neighbour):
        return pltpu.make_async_remote_copy(
            src_ref=source, dst_ref=target,
            send_sem=hop_send.at[index], recv_sem=hop_recv.at[index],
            device_id={"section": neighbour}, device_id_type=MESH,
        )

    grad_hop = hop(0, grad_ref, cot, before)
    act_hop = hop(1, act_ref, arrived, after)
    gain = gain_ref[...].astype(F32)
    experts = router_ref.shape[0]
    router = jnp.concatenate(
        [router_ref[...].astype(F32), jnp.zeros((LANES - experts, width), F32)], axis=0
    ).astype(BF16)
    ones = [1.0] * top

    match_b, pos_b = places(routes_b_ref[...], top, capacity)
    values = stored_ref[...].astype(F32)
    inverse_b = inverse_rms(values)
    normed[...] = (values * inverse_b * gain).astype(BF16)
    spread_b = table(pos_b, ones, slots).T.astype(BF16)

    def fill_b(cols):
        send_b[:, cols] = mm(spread_b, normed[:, cols]).astype(BF16)

    chunks(0, half, CHUNK, fill_b)
    pl.semaphore_wait(barrier, owners + 1)
    send(ROW_B, 0)
    grad_hop.start()
    chunks(half, width, CHUNK, fill_b)
    send(ROW_B, 1)
    weights_b, sig_b, total_b = route_weights(normed[...], router, match_b)
    scales = [w.astype(BF16).astype(F32) for w in weights_b]
    scale_table = table(pos_b, scales, slots).T.astype(BF16)
    send_c[:, width:] = mm(scale_table, jnp.ones((scale_table.shape[1], LANES), BF16)).astype(BF16)

    grad_hop.wait()
    act_hop.start()

    def fill_c(cols):
        send_c[:, cols] = mm(spread_b, cot[:, cols]).astype(BF16)

    fill_and_send(ROW_C, fill_c)

    def expert_hidden(rows_ref, keep):
        def work(cols):
            g = mm(rows_ref[...], gate_w[:, cols])
            u = mm(rows_ref[...], up_w[:, cols])
            if keep:
                gate[:, cols] = g
                upper[:, cols] = u
            hidden[:, cols] = (g * jax.nn.sigmoid(g) * u).astype(BF16)

        chunks(0, hidden_width, CHUNK, work)

    def expert_down(target):
        def work(cols):
            target[:, cols] = mm(hidden[...], down_w[:, cols]).astype(BF16)

        return work

    match_f, pos_f = places(routes_f_ref[...], top, capacity)
    spread_f = table(pos_f, ones, slots).T.astype(BF16)
    act_hop.wait()
    values = arrived[...].astype(F32)
    normed[...] = (values * inverse_rms(values) * gain).astype(BF16)

    def fill_f(cols):
        send_f[:, cols] = mm(spread_f, normed[:, cols]).astype(BF16)

    chunks(0, width, CHUNK, fill_f)
    weights_f = route_weights(normed[...], router, match_f)[0]
    for load in loads:
        load.wait()
    for part in range(2):
        receive(ROW_B, part)
    for part in range(2):
        send(ROW_F, part)
    expert_hidden(recv_b, True)
    chunks(0, width, CHUNK, expert_down(out_b))

    for part in range(2):
        receive(ROW_C, part)
    acc[...] = jnp.zeros_like(acc)
    scale = recv_c[:, width:].astype(F32)[:, :1]

    def scale_rows(cols):
        rows = recv_c[:, cols].astype(F32)
        slot_grad[:, cols] = (scale * rows).astype(BF16)
        product = rows * out_b[:, cols].astype(F32)
        acc[...] += product[:, :LANES] + product[:, LANES:]

    chunks(0, width, CHUNK, scale_rows)
    scores = jnp.sum(acc[...], axis=1, keepdims=True)
    send_g[:, width:] = jnp.broadcast_to(scores, (slots, LANES)).astype(BF16)

    def hidden_grads(cols):
        grad_hidden = mm(slot_grad[...], down_w[cols, :], NT)
        g = gate[:, cols]
        s = jax.nn.sigmoid(g)
        grad_up[:, cols] = (grad_hidden * g * s).astype(BF16)
        grad_gate[:, cols] = (
            grad_hidden * upper[:, cols] * s * (1.0 + g * (1.0 - s))
        ).astype(BF16)

    chunks(0, hidden_width, CHUNK, hidden_grads)

    def row_grads(cols):
        total = mm(grad_gate[...], gate_w[cols, :], NT) + mm(grad_up[...], up_w[cols, :], NT)
        send_g[:, cols] = total.astype(BF16)

    fill_and_send(OUT_G, row_grads)

    for part in range(2):
        receive(ROW_F, part)
    expert_hidden(recv_f, False)
    fill_and_send(OUT_F, expert_down(send_o))

    for part in range(2):
        receive(OUT_G, part)
    score = [
        mm(table([p], [1.0], slots).astype(BF16), recv_g[:, width:])[:, :1] for p in pos_b
    ]
    mixed = sum(w * s for w, s in zip(weights_b, score))
    grad_logits = sum(
        (s - mixed) / total_b * g * (1.0 - g) * m for s, g, m in zip(score, sig_b, match_b)
    )
    logits_high, logits_low = halves(grad_logits)
    gather_b = table(pos_b, ones, slots).astype(BF16)
    grad_normed = (
        mm(gather_b, recv_g[:, :width])
        + mm(logits_high, router)
        + mm(logits_low, router)
    )
    grad_pre = grad_normed * gain
    values = stored_ref[...].astype(F32)
    mean = jnp.mean(grad_pre * values, axis=1, keepdims=True)
    input_ref[...] = (
        cot[...].astype(F32)
        + inverse_b * grad_pre
        - values * (inverse_b * inverse_b * inverse_b) * mean
    ).astype(BF16)

    weight_high, weight_low = halves(table(pos_f, weights_f, slots))

    def combine(cols):
        rows = recv_o[:, cols]
        mixed_rows = mm(weight_high, rows) + mm(weight_low, rows)
        layer_ref[:, cols] = (arrived[:, cols].astype(F32) + mixed_rows).astype(BF16)

    for part in range(2):
        receive(OUT_F, part)
        chunks(part * half, (part + 1) * half, CHUNK, combine)

    for kind in range(5):
        for part in range(2):

            @pl.loop(1, owners)
            def _(step, kind=kind, part=part):
                block_copy(kind, part, step).wait_send()


def hand_over(layer_in, grad_in, layer_ref, input_ref, sem):
    count = sem.shape[1]
    share = layer_in.shape[0] // count
    copies = [
        pltpu.make_async_copy(
            source.at[pl.ds(i * share, share)], target.at[pl.ds(i * share, share)], sem.at[j, i]
        )
        for j, (source, target) in enumerate(((layer_in, layer_ref), (grad_in, input_ref)))
        for i in range(count)
    ]
    for copy in copies:
        copy.start()
    for copy in copies:
        copy.wait()


def body(
    activations, gradients, stashed, norm_gain, router,
    gate_weight, up_weight, down_weight, routes_forward, routes_backward,
):
    owners, sections = lax.axis_size("expert"), lax.axis_size("section")
    rows, width = activations.shape[1:]
    top = routes_forward.shape[2]
    hidden_width = gate_weight.shape[3]
    capacity = 3 * rows * top // (2 * owners)
    capacity = -(-capacity // 16) * 16
    slots = owners * capacity
    vmem, hbm = pl.BlockSpec(memory_space=pltpu.VMEM), pl.BlockSpec(memory_space=pl.ANY)
    plain, wide = pltpu.VMEM((slots, width), BF16), pltpu.VMEM((slots, width + LANES), BF16)
    inner = pltpu.VMEM((slots, hidden_width), BF16)
    inner_f32 = pltpu.VMEM((slots, hidden_width), F32)
    tokens = pltpu.VMEM((rows, width), BF16)
    layer_out, input_grad = pl.pallas_call(
        functools.partial(kernel, owners, sections, capacity, top),
        out_shape=[jax.ShapeDtypeStruct((rows, width), BF16)] * 2,
        in_specs=[vmem] * 7 + [hbm] * 3,
        out_specs=[vmem] * 2,
        scratch_shapes=[
            pltpu.VMEM((width, hidden_width), BF16),
            pltpu.VMEM((width, hidden_width), BF16),
            pltpu.VMEM((hidden_width, width), BF16),
            tokens, tokens,
            plain, wide, plain, wide, plain,
            plain, wide, plain, wide, plain,
            tokens, inner_f32, inner_f32, inner, plain, plain, inner, inner,
            pltpu.VMEM((slots, LANES), F32),
            pltpu.SemaphoreType.DMA((3,)),
            pltpu.SemaphoreType.DMA((2,)),
            pltpu.SemaphoreType.DMA((2,)),
            pltpu.SemaphoreType.DMA((10, owners)),
            pltpu.SemaphoreType.DMA((10, owners)),
        ],
        compiler_params=pltpu.CompilerParams(
            collective_id=0, has_side_effects=True, vmem_limit_bytes=58 << 20
        ),
        cost_estimate=pl.CostEstimate(
            flops=18 * slots * width * hidden_width,
            bytes_accessed=6 * width * hidden_width + 10 * rows * width,
            transcendentals=3 * slots * hidden_width,
        ),
    )(
        activations[0], gradients[0], stashed[0], norm_gain, router[0].T,
        routes_forward[0].T, routes_backward[0].T,
        gate_weight[0, 0], up_weight[0, 0], down_weight[0, 0],
    )
    layer_out, input_grad = pl.pallas_call(
        hand_over,
        out_shape=[jax.ShapeDtypeStruct((rows, width), BF16)] * 2,
        in_specs=[hbm] * 2,
        out_specs=[hbm] * 2,
        scratch_shapes=[pltpu.SemaphoreType.DMA((2, 4))],
    )(layer_out, input_grad)
    return layer_out[None], input_grad[None]


def solution(mesh):
    rows = P("section", "expert", None)
    experts = P("section", "expert", None, None)
    placed = (
        rows, rows, rows, P("section", None), P("section", None, None),
        experts, experts, experts, rows, rows,
    )
    return jax.shard_map(
        body, mesh=mesh, in_specs=placed, out_specs=(rows, rows), check_vma=False
    )
```

```python
import functools

import jax
import jax.numpy as jnp
from jax import lax
from jax.experimental import pallas as pl
from jax.experimental.pallas import tpu as pltpu
from jax.sharding import PartitionSpec as P

NORM_EPS = 1e-06
LANES = 128
CHUNK = 256
F32, BF16 = jnp.float32, jnp.bfloat16
MESH = pl.DeviceIdType.MESH
NN = (((1,), (0,)), ((), ()))
NT = (((1,), (1,)), ((), ()))
ROW_B, ROW_C, ROW_F, OUT_G, OUT_F = range(5)


def mm(left, right, dims=NN):
    return lax.dot_general(left, right, dims, preferred_element_type=F32)


def halves(value):
    high = value.astype(BF16)
    return high, (value - high.astype(F32)).astype(BF16)


def chunks(width, step, work):
    @pl.loop(0, width // step)
    def _(index):
        work(pl.ds(pl.multiple_of(index * step, step), step))


def inverse_rms(values):
    return lax.rsqrt(jnp.mean(values * values, axis=1, keepdims=True) + NORM_EPS)


def places(routes, top, capacity):
    rows = routes.shape[1]
    columns = lax.broadcasted_iota(jnp.int32, (rows, LANES), 1).astype(F32)
    across = lax.broadcasted_iota(jnp.int32, (rows, rows), 1)
    down = lax.broadcasted_iota(jnp.int32, (rows, rows), 0)
    named = [
        jnp.sum(
            jnp.where(across == down, routes[k : k + 1, :].astype(F32), 0.0),
            axis=1, keepdims=True,
        )
        for k in range(top)
    ]
    matches = [(n == columns).astype(F32) for n in named]
    per_row = sum(matches)
    before = across < down
    earlier = mm(before.astype(F32).astype(BF16), per_row.astype(BF16))
    offsets = earlier + columns * capacity
    return matches, [jnp.sum(m * offsets, axis=1, keepdims=True) for m in matches]


def route_weights(normed, router, matches):
    logits = mm(normed, router, NT)
    sig = [jax.nn.sigmoid(jnp.sum(m * logits, axis=1, keepdims=True)) for m in matches]
    total = sum(sig)
    return [s / total for s in sig], sig, total


def table(positions, scales, slots):
    rows = positions[0].shape[0]
    columns = lax.broadcasted_iota(jnp.int32, (rows, slots), 1).astype(F32)
    return sum(jnp.where(columns == p, s, 0.0) for p, s in zip(positions, scales))


def kernel(
    owners, sections, capacity, top,
    act_ref, grad_ref, stored_ref, gain_ref, router_ref, routes_f_ref, routes_b_ref,
    gate_hbm, up_hbm, down_hbm,
    layer_ref, input_ref,
    gate_w, up_w, down_w, arrived, cot,
    send_b, send_c, send_f, send_g, send_o,
    recv_b, recv_c, recv_f, recv_g, recv_o,
    normed, gate, upper, hidden, slot_grad, out_b, grad_gate, grad_up, acc,
    weight_sem, hop_send, hop_recv, send_sem, recv_sem,
):
    slots = owners * capacity
    width = act_ref.shape[1]
    hidden_width = gate_w.shape[1]
    me = lax.axis_index("expert")
    section = lax.axis_index("section")
    after = lax.rem(section + 1, sections)
    before = lax.rem(section + sections - 1, sections)
    sends = (send_b, send_c, send_f, send_g, send_o)
    recvs = (recv_b, recv_c, recv_f, recv_g, recv_o)

    loads = [
        pltpu.make_async_copy(source, target, weight_sem.at[i])
        for i, (source, target) in enumerate(
            ((gate_hbm, gate_w), (up_hbm, up_w), (down_hbm, down_w))
        )
    ]
    for load in loads:
        load.start()

    barrier = pltpu.get_barrier_semaphore()

    @pl.loop(1, owners)
    def _(step):
        pl.semaphore_signal(
            barrier, inc=1, device_id={"expert": lax.rem(me + step, owners)}, device_id_type=MESH
        )

    for neighbour in (after, before):
        pl.semaphore_signal(barrier, inc=1, device_id={"section": neighbour}, device_id_type=MESH)
    def rows_of(index):
        return pl.ds(pl.multiple_of(index * capacity, 16), capacity)

    def block_copy(kind, step):
        peer = lax.rem(me + step, owners)
        return pltpu.make_async_remote_copy(
            src_ref=sends[kind].at[rows_of(peer)],
            dst_ref=recvs[kind].at[rows_of(me)],
            send_sem=send_sem.at[kind, step],
            recv_sem=recv_sem.at[kind, step],
            device_id={"expert": peer},
            device_id_type=MESH,
        )

    def send(kind):
        @pl.loop(1, owners)
        def _(step):
            block_copy(kind, step).start()

        recvs[kind][rows_of(me)] = sends[kind][rows_of(me)]

    def receive(kind):
        @pl.loop(1, owners)
        def _(step):
            source = lax.rem(me + owners - step, owners)
            pltpu.make_async_remote_copy(
                src_ref=sends[kind].at[rows_of(source)],
                dst_ref=recvs[kind].at[rows_of(source)],
                send_sem=send_sem.at[kind, step],
                recv_sem=recv_sem.at[kind, step],
                device_id={"expert": source},
                device_id_type=MESH,
            ).wait_recv()

    def hop(index, source, target, neighbour):
        return pltpu.make_async_remote_copy(
            src_ref=source, dst_ref=target,
            send_sem=hop_send.at[index], recv_sem=hop_recv.at[index],
            device_id={"section": neighbour}, device_id_type=MESH,
        )

    grad_hop = hop(0, grad_ref, cot, before)
    act_hop = hop(1, act_ref, arrived, after)
    gain = gain_ref[...].astype(F32)
    experts = router_ref.shape[0]
    router = jnp.concatenate(
        [router_ref[...].astype(F32), jnp.zeros((LANES - experts, width), F32)], axis=0
    ).astype(BF16)
    ones = [1.0] * top

    match_b, pos_b = places(routes_b_ref[...], top, capacity)
    values = stored_ref[...].astype(F32)
    inverse_b = inverse_rms(values)
    normed[...] = (values * inverse_b * gain).astype(BF16)
    spread_b = table(pos_b, ones, slots).T.astype(BF16)

    def fill_b(cols):
        send_b[:, cols] = mm(spread_b, normed[:, cols]).astype(BF16)

    chunks(width, CHUNK, fill_b)
    pl.semaphore_wait(barrier, owners + 1)
    grad_hop.start()
    send(ROW_B)
    weights_b, sig_b, total_b = route_weights(normed[...], router, match_b)
    scales = [w.astype(BF16).astype(F32) for w in weights_b]
    scale_table = table(pos_b, scales, slots).T.astype(BF16)
    send_c[:, width:] = mm(scale_table, jnp.ones((scale_table.shape[1], LANES), BF16)).astype(BF16)

    grad_hop.wait()
    act_hop.start()

    def fill_c(cols):
        send_c[:, cols] = mm(spread_b, cot[:, cols]).astype(BF16)

    chunks(width, CHUNK, fill_c)
    send(ROW_C)

    def expert_hidden(rows_ref, keep):
        def work(cols):
            g = mm(rows_ref[...], gate_w[:, cols])
            u = mm(rows_ref[...], up_w[:, cols])
            if keep:
                gate[:, cols] = g
                upper[:, cols] = u
            hidden[:, cols] = (g * jax.nn.sigmoid(g) * u).astype(BF16)

        chunks(hidden_width, CHUNK, work)

    def expert_down(target):
        def work(cols):
            target[:, cols] = mm(hidden[...], down_w[:, cols]).astype(BF16)

        chunks(width, CHUNK, work)

    match_f, pos_f = places(routes_f_ref[...], top, capacity)
    spread_f = table(pos_f, ones, slots).T.astype(BF16)
    act_hop.wait()
    values = arrived[...].astype(F32)
    normed[...] = (values * inverse_rms(values) * gain).astype(BF16)

    def fill_f(cols):
        send_f[:, cols] = mm(spread_f, normed[:, cols]).astype(BF16)

    chunks(width, CHUNK, fill_f)
    weights_f = route_weights(normed[...], router, match_f)[0]
    for load in loads:
        load.wait()
    send(ROW_F)
    receive(ROW_B)
    expert_hidden(recv_b, True)
    expert_down(out_b)

    receive(ROW_C)
    acc[...] = jnp.zeros_like(acc)
    scale = recv_c[:, width:].astype(F32)[:, :1]

    def scale_rows(cols):
        rows = recv_c[:, cols].astype(F32)
        slot_grad[:, cols] = (scale * rows).astype(BF16)
        product = rows * out_b[:, cols].astype(F32)
        acc[...] += product[:, :LANES] + product[:, LANES:]

    chunks(width, CHUNK, scale_rows)

    def hidden_grads(cols):
        grad_hidden = mm(slot_grad[...], down_w[cols, :], NT)
        g = gate[:, cols]
        s = jax.nn.sigmoid(g)
        grad_up[:, cols] = (grad_hidden * g * s).astype(BF16)
        grad_gate[:, cols] = (
            grad_hidden * upper[:, cols] * s * (1.0 + g * (1.0 - s))
        ).astype(BF16)

    chunks(hidden_width, CHUNK, hidden_grads)

    def row_grads(cols):
        total = mm(grad_gate[...], gate_w[cols, :], NT) + mm(grad_up[...], up_w[cols, :], NT)
        send_g[:, cols] = total.astype(BF16)

    chunks(width, CHUNK, row_grads)
    scores = jnp.sum(acc[...], axis=1, keepdims=True)
    send_g[:, width:] = jnp.broadcast_to(scores, (slots, LANES)).astype(BF16)
    send(OUT_G)

    receive(ROW_F)
    expert_hidden(recv_f, False)
    expert_down(send_o)
    send(OUT_F)

    receive(OUT_G)
    score = [
        mm(table([p], [1.0], slots).astype(BF16), recv_g[:, width:])[:, :1] for p in pos_b
    ]
    mixed = sum(w * s for w, s in zip(weights_b, score))
    grad_logits = sum(
        (s - mixed) / total_b * g * (1.0 - g) * m for s, g, m in zip(score, sig_b, match_b)
    )
    logits_high, logits_low = halves(grad_logits)
    gather_b = table(pos_b, ones, slots).astype(BF16)
    grad_normed = (
        mm(gather_b, recv_g[:, :width])
        + mm(logits_high, router)
        + mm(logits_low, router)
    )
    grad_pre = grad_normed * gain
    values = stored_ref[...].astype(F32)
    mean = jnp.mean(grad_pre * values, axis=1, keepdims=True)
    input_ref[...] = (
        cot[...].astype(F32)
        + inverse_b * grad_pre
        - values * (inverse_b * inverse_b * inverse_b) * mean
    ).astype(BF16)

    weight_high, weight_low = halves(table(pos_f, weights_f, slots))
    receive(OUT_F)

    def combine(cols):
        rows = recv_o[:, cols]
        mixed_rows = mm(weight_high, rows) + mm(weight_low, rows)
        layer_ref[:, cols] = (arrived[:, cols].astype(F32) + mixed_rows).astype(BF16)

    chunks(width, CHUNK, combine)

    for kind in range(5):

        @pl.loop(1, owners)
        def _(step, kind=kind):
            block_copy(kind, step).wait_send()


def hand_over(layer_in, grad_in, layer_ref, input_ref):
    layer_ref[...] = layer_in[...]
    input_ref[...] = grad_in[...]


def body(
    activations, gradients, stashed, norm_gain, router,
    gate_weight, up_weight, down_weight, routes_forward, routes_backward,
):
    owners, sections = lax.axis_size("expert"), lax.axis_size("section")
    rows, width = activations.shape[1:]
    top = routes_forward.shape[2]
    hidden_width = gate_weight.shape[3]
    capacity = 3 * rows * top // (2 * owners)
    capacity = -(-capacity // 16) * 16
    slots = owners * capacity
    vmem, hbm = pl.BlockSpec(memory_space=pltpu.VMEM), pl.BlockSpec(memory_space=pl.ANY)
    plain, wide = pltpu.VMEM((slots, width), BF16), pltpu.VMEM((slots, width + LANES), BF16)
    inner = pltpu.VMEM((slots, hidden_width), BF16)
    inner_f32 = pltpu.VMEM((slots, hidden_width), F32)
    tokens = pltpu.VMEM((rows, width), BF16)
    layer_out, input_grad = pl.pallas_call(
        functools.partial(kernel, owners, sections, capacity, top),
        out_shape=[jax.ShapeDtypeStruct((rows, width), BF16)] * 2,
        in_specs=[vmem] * 7 + [hbm] * 3,
        out_specs=[vmem] * 2,
        scratch_shapes=[
            pltpu.VMEM((width, hidden_width), BF16),
            pltpu.VMEM((width, hidden_width), BF16),
            pltpu.VMEM((hidden_width, width), BF16),
            tokens, tokens,
            plain, wide, plain, wide, plain,
            plain, wide, plain, wide, plain,
            tokens, inner_f32, inner_f32, inner, plain, plain, inner, inner,
            pltpu.VMEM((slots, LANES), F32),
            pltpu.SemaphoreType.DMA((3,)),
            pltpu.SemaphoreType.DMA((2,)),
            pltpu.SemaphoreType.DMA((2,)),
            pltpu.SemaphoreType.DMA((5, owners)),
            pltpu.SemaphoreType.DMA((5, owners)),
        ],
        compiler_params=pltpu.CompilerParams(
            collective_id=0, has_side_effects=True, vmem_limit_bytes=58 << 20
        ),
        cost_estimate=pl.CostEstimate(
            flops=18 * slots * width * hidden_width,
            bytes_accessed=6 * width * hidden_width + 10 * rows * width,
            transcendentals=3 * slots * hidden_width,
        ),
    )(
        activations[0], gradients[0], stashed[0], norm_gain, router[0].T,
        routes_forward[0].T, routes_backward[0].T,
        gate_weight[0, 0], up_weight[0, 0], down_weight[0, 0],
    )
    layer_out, input_grad = pl.pallas_call(
        hand_over,
        out_shape=[jax.ShapeDtypeStruct((rows, width), BF16)] * 2,
        in_specs=[vmem] * 2,
        out_specs=[vmem] * 2,
    )(layer_out, input_grad)
    return layer_out[None], input_grad[None]


def solution(mesh):
    rows = P("section", "expert", None)
    experts = P("section", "expert", None, None)
    placed = (
        rows, rows, rows, P("section", None), P("section", None, None),
        experts, experts, experts, rows, rows,
    )
    return jax.shard_map(
        body, mesh=mesh, in_specs=placed, out_specs=(rows, rows), check_vma=False
    )
```
